256 devices in a mesh: pole: 8 (over z), row: 4 (over x_hi, core), col: 8 (over y, x_lo).
Axes of the slice: x: 4 (x_hi: 2, x_lo: 2; x = x_hi * 2 + x_lo), y: 4, z: 8, core: 2. Of those that a mesh axis runs over, the one named last changes fastest.
Arguments:
- ainv: float32 [8, 8192, 8192], P('pole', 'row', 'col'), may hold values from -6 to 6
- lfac: float32 [8, 8192, 384], P('pole', ('row', 'col')), may hold values from -0.0625 to 0.0625
- dinv: float32 [8, 384, 384], P('pole'), may hold values from -6 to 6
- weights: float32 [8], P('pole'), may hold values from 0.1 to 1
- present: int32 [32], replicated, may hold values 0 or 1
Outputs:
- ainv_col: float32 [8, 8192, 384], P('pole', ('row', 'col'))
- ainv_diag: float32 [8, 384, 384], P('pole')
- dm_col: float32 [8192, 384], P(('row', 'col'))
- dm_diag: float32 [384, 384], replicated
The draws below stay inside these ranges and needn't reach their ends.
All inputs are finite; a program needn't handle non-finite values.
Results may differ from the reference program's by a relative error of at most 0.000071.
Values sent between devices are 32-bit elements; how exact they have to be, the bound alone decides.
No kernel may reach another device: no remote copies, remote signals or barrier semaphores. Data moves between devices by JAX's collectives and lax.ppermute only.
A program may use at most 128 MiB of HBM per device.

```python
import math
import jax
import jax.numpy as jnp
from jax import lax

SUPER = 384
ROWS_DEV = 256
NBLK = 32
STRUCT = 8192
N_POLE = 8


def with_ends(values, rng, least, largest):
    longest = values.shape.index(max(values.shape))
    spots = []
    for shift in (0, 1):
        where = [jax.random.randint(jax.random.fold_in(rng, axis), (), 0, length) for axis, length in enumerate(values.shape)]
        where[longest] = (where[longest] + shift) % values.shape[longest]
        spots.append(tuple(where))
    return values.at[spots[0]].set(least).at[spots[1]].set(largest)


def levels(rng, extent, shards, least, top_value):
    def one(position, shards_of):
        draws = jax.random.uniform(jax.random.fold_in(jax.random.fold_in(rng, 6), position), (shards_of,), jnp.float32, least / len(shards), top_value / len(shards))
        return jnp.repeat(jnp.exp(draws), extent[position] // shards_of).reshape((-1,) + (1,) * (len(extent) - position - 1))

    loudness = one(*shards[0])
    for cut in shards[1:]:
        loudness = loudness * one(*cut)
    return loudness


def centred(own_key, shape, spread, bound, split=(), held_as=jnp.bfloat16):
    values = spread * jax.random.normal(own_key, shape, jnp.float32)
    if split:
        values = values * levels(own_key, shape, split, -0.22, 0.18)
    return jnp.clip(values, -bound, bound).astype(held_as)


def setup_inputs(seed: int = 0) -> dict:
    key_list = jax.random.split(jax.random.key(seed), 6)
    return {
        "ainv": centred(key_list[0], (N_POLE, STRUCT, STRUCT), 1.0, 6.0, ((0, 8), (1, 4), (2, 8)), jnp.float32),
        "lfac": centred(key_list[1], (N_POLE, STRUCT, SUPER), STRUCT ** -0.5, 0.0625, ((0, 8), (1, 32)), jnp.float32),
        "dinv": centred(key_list[2], (N_POLE, SUPER, SUPER), 1.0, 6.0, ((0, 8),), jnp.float32),
        "weights": jnp.clip(jnp.exp(math.log(1.0) - 2.3025851 * jax.random.uniform(key_list[3], (N_POLE,), jnp.float32) ** levels(key_list[3], (N_POLE,), ((0, 8),), -0.2, 0.2)), 0.1, 1.0),
        "present": with_ends((jax.random.randint(key_list[4], (NBLK,), 0, 4) < 3).astype(jnp.int32), jax.random.fold_in(key_list[4], 1), 0, 1),
    }


def reference(ainv, lfac, dinv, weights, present):
    rows_present = jnp.repeat(present.astype(jnp.float32), ROWS_DEV)[:, None]

    def one_pole(items):
        inverse, factor, diag_inverse = items
        masked = factor * rows_present
        column_block = -(rows_present * jnp.dot(inverse, masked, precision=lax.Precision.HIGHEST, preferred_element_type=jnp.float32))
        diagonal = diag_inverse - jnp.dot(masked.T, column_block, precision=lax.Precision.HIGHEST, preferred_element_type=jnp.float32)
        return column_block, diagonal

    columns, diagonals = lax.map(one_pole, (ainv, lfac, dinv))
    dm_col = jnp.sum(weights[:, None, None] * columns, axis=0)
    dm_diag = jnp.sum(weights[:, None, None] * diagonals, axis=0)
    return columns, diagonals, dm_col, dm_diag
```

```python
import jax
import jax.numpy as jnp
from jax import lax
from jax.experimental import pallas as pl
from jax.experimental.pallas import tpu as pltpu
from jax.sharding import PartitionSpec as P

PLANE = ("row", "col")
MIB = 1 << 20


def place(x, y, core):
    return ((x // 2) * 2 + core) * 8 + y * 2 + x % 2


CHIPS = [(x, y, core) for x in range(4) for y in range(4) for core in range(2)]


def shift(value, dx=0, dy=0, other=0):
    pairs = [(place(x, y, c), place((x + dx) % 4, (y + dy) % 4, c ^ other)) for x, y, c in CHIPS]
    return lax.ppermute(value, PLANE, pairs)


def flip_x(value):
    return lax.ppermute(value, PLANE, [(place(x, y, c), place(x ^ 1, y, c)) for x, y, c in CHIPS])


def along_pole(value, step):
    return lax.ppermute(value, "pole", [(z, (z + step) % 8) for z in range(8)])


def pole_pair(value):
    return lax.ppermute(value, "pole", [(z, z ^ 1) for z in range(8)])


def panel_slot(value, j):
    pairs = []
    for x, y, c in CHIPS:
        k = 2 * c + (j ^ (x // 2))
        source = place((y // 2) * 2 + k % 2, 2 * (x % 2) + k // 2, y % 2)
        pairs.append((source, place(x, y, c)))
    return lax.ppermute(value, PLANE, pairs)


def split(value):
    high = value.astype(jnp.bfloat16)
    return high, (value - high.astype(jnp.float32)).astype(jnp.bfloat16)


def mm(a, b, contract=((1,), (0,))):
    return lax.dot_general(a, b, (contract, ((), ())), preferred_element_type=jnp.float32)


def mm3(a_high, a_low, b_high, b_low, contract=((1,), (0,))):
    return mm(a_high, b_high, contract) + (mm(a_high, b_low, contract) + mm(a_low, b_high, contract))


def first_kernel(info, inverse, s0, s1, t0, t1, out, high, low):
    rows = s0.shape[0]

    @pl.when(pl.program_id(0) == 0)
    def _():
        for i, slot in enumerate((s0, s1, t0, t1)):
            at = pl.ds(pl.multiple_of(info[1 + i] * rows, rows), rows)
            keep = (info[5 + i] > 0).astype(jnp.float32)
            high[at, :], low[at, :] = split(slot[...] * keep)

    out[...] = mm3(*split(inverse[...]), high[...], low[...])


def next_kernel(info, inverse, high, low, out):
    out[...] = mm3(*split(inverse[...]), high[...], low[...])


def chunk_dot(info, inverse, panel, rows, tile=256):
    depth = inverse.shape[1]
    width = panel[0].shape[1]
    first = len(panel) == 4
    steps = 2 * rows // tile
    whole = pl.BlockSpec(memory_space=pltpu.VMEM)
    out_shape = [jax.ShapeDtypeStruct((2 * rows, width), jnp.float32)]
    out_specs = [pl.BlockSpec((tile, width), lambda i, info: (i, 0))]
    if first:
        out_shape += [jax.ShapeDtypeStruct((depth, width), jnp.bfloat16)] * 2
        out_specs += [whole] * 2
    return pl.pallas_call(
        first_kernel if first else next_kernel,
        out_shape=out_shape,
        grid_spec=pltpu.PrefetchScalarGridSpec(
            num_scalar_prefetch=1,
            grid=(steps,),
            in_specs=[pl.BlockSpec((tile, depth), lambda i, info: (info[0] * steps + i, 0))]
            + [whole] * len(panel),
            out_specs=out_specs,
        ),
        cost_estimate=pl.CostEstimate(
            flops=6 * 2 * rows * depth * width,
            bytes_accessed=4 * (2 * rows * depth + 2 * rows * width + depth * width),
            transcendentals=0,
        ),
        compiler_params=pltpu.CompilerParams(vmem_limit_bytes=32 * MIB),
    )(info, inverse, *panel)


def corr_kernel(info, p0, u_first, u_second, d_first, d_second, own, other, corr, s_own, s_other):
    rows = own.shape[0]
    at_own, at_other = info[0], info[1]
    first = p0[:rows] + (u_first[...] + d_first[...])
    second = p0[rows:] + (u_second[...] + d_second[...])
    own_is_first = at_own == 0
    sum_own = jnp.where(own_is_first, first, second)
    sum_other = jnp.where(own_is_first, second, first)
    keep_own = (info[2] > 0).astype(jnp.float32)
    keep_other = (info[3] > 0).astype(jnp.float32)
    sum_own = sum_own * keep_own
    sum_other = sum_other * keep_other
    s_own[...] = sum_own
    s_other[...] = sum_other
    by_rows = ((0,), (0,))
    corr[...] = mm3(*split(own[...]), *split(sum_own), by_rows) + mm3(
        *split(other[...]), *split(sum_other), by_rows
    )


def correction(info, *arrays):
    rows, width = arrays[-1].shape
    vmem = pl.BlockSpec(memory_space=pltpu.VMEM)
    return pl.pallas_call(
        corr_kernel,
        out_shape=[
            jax.ShapeDtypeStruct((width, width), jnp.float32),
            jax.ShapeDtypeStruct((rows, width), jnp.float32),
            jax.ShapeDtypeStruct((rows, width), jnp.float32),
        ],
        in_specs=[pl.BlockSpec(memory_space=pltpu.SMEM)] + [vmem] * len(arrays),
        out_specs=[vmem] * 3,
        cost_estimate=pl.CostEstimate(
            flops=12 * rows * width * width, bytes_accessed=36 * rows * width, transcendentals=0
        ),
        compiler_params=pltpu.CompilerParams(vmem_limit_bytes=32 * MIB),
    )(info, *arrays)


def part(value, index, size):
    return lax.dynamic_slice_in_dim(value, index * size, size, 0)


def ring_scatter(value, me, size, send):
    away = [send(part(value, (me + k) % 4, size), k) for k in (1, 2, 3)]
    return (part(value, me, size) + away[1]) + (away[0] + away[2])


def ring_gather(value, me, send):
    size = value.shape[0]
    rising = [send(value, 3), send(value, 2), send(value, 1), value]
    twice = jnp.concatenate(rising + rising[:3], 0)
    return lax.dynamic_slice_in_dim(twice, (3 - me) * size, 4 * size, 0)


def pair_gather(value, me, swap):
    other = swap(value)
    size = value.shape[0]
    thrice = jnp.concatenate([other, value, other], 0)
    return lax.dynamic_slice_in_dim(thrice, (1 - me) * size, 2 * size, 0)


def on_device(ainv, lfac, dinv, weights, present):
    own = lfac[0]
    rows, width = own.shape
    row, col = lax.axis_index("row"), lax.axis_index("col")
    z = lax.axis_index("pole")
    x_hi, core = row // 2, row % 2
    y, x_lo = col // 2, col % 2
    x = x_hi * 2 + x_lo
    half, quarter = width // 2, width // 8

    def sibling(v):
        return shift(v, other=1)

    slots = [panel_slot(own, 0), panel_slot(own, 1)]
    slots += [sibling(s) for s in slots]
    other = flip_x(own)
    order = jnp.stack([2 * core + x_hi, 2 * core + 1 - x_hi, 2 * (1 - core) + x_hi, 2 * (1 - core) + 1 - x_hi])
    kept = jnp.take(present, 4 * col + order)

    def info(d):
        return jnp.concatenate([((y + d) % 4)[None], order, kept]).astype(jnp.int32)

    inverse = ainv[0]
    p2, high, low = chunk_dot(info(2), inverse, slots, rows)
    r_up = shift(p2[:rows], dy=1)
    r_down = shift(p2[rows:], dy=-1)
    (p1,) = chunk_dot(info(1), inverse, (high, low), rows)
    u_second = shift(p1[rows:], dy=1)
    (p3,) = chunk_dot(info(3), inverse, (high, low), rows)
    d_first = shift(p3[:rows], dy=-1)
    (p0,) = chunk_dot(info(0), inverse, (high, low), rows)
    u_first = shift(p1[:rows] + r_up, dy=1)
    d_second = shift(p3[rows:] + r_down, dy=-1)

    keep = jnp.take(present, row * 8 + jnp.stack([col, col ^ 1]))
    tail = jnp.concatenate([jnp.stack([x_lo, 1 - x_lo]), keep]).astype(jnp.int32)
    corr, s_own, s_other = correction(tail, p0, u_first, u_second, d_first, d_second, own, other)

    column = -(s_own + flip_x(s_other))

    mine = part(corr, core, half) + sibling(part(corr, 1 - core, half))
    mine = ring_scatter(mine, x, quarter, lambda v, k: shift(v, dx=k))
    mine = (mine + shift(mine, dy=2)) + (shift(mine, dy=1) + shift(mine, dy=3))
    diagonal = lax.dynamic_slice_in_dim(dinv[0], core * half + x * quarter, quarter, 0) + mine

    def spread(v):
        v = ring_gather(v, x, lambda u, k: shift(u, dx=k))
        return pair_gather(v, core, sibling)

    weight = weights[0]
    part_dm = weight * diagonal
    part_dm = part_dm + pole_pair(part_dm)
    part_dm = (part_dm + along_pole(part_dm, 4)) + (along_pole(part_dm, 2) + along_pole(part_dm, 6))

    pair, four = z % 2, z // 2
    weighted = weight * column
    dm = part(weighted, pair, rows // 2) + pole_pair(part(weighted, 1 - pair, rows // 2))
    dm = ring_scatter(dm, four, rows // 8, lambda v, k: along_pole(v, 2 * k))
    dm = ring_gather(dm, four, lambda v, k: along_pole(v, 2 * k))
    dm = pair_gather(dm, pair, pole_pair)

    return column[None], spread(diagonal)[None], dm, spread(part_dm)


def solution(mesh):
    return jax.shard_map(
        on_device,
        mesh=mesh,
        in_specs=(
            P("pole", "row", "col"),
            P("pole", ("row", "col"), None),
            P("pole", None, None),
            P("pole"),
            P(),
        ),
        out_specs=(
            P("pole", ("row", "col"), None),
            P("pole", None, None),
            P(("row", "col"), None),
            P(),
        ),
        check_vma=False,
    )
```

```python
import jax
import jax.numpy as jnp
from jax import lax
from jax.experimental import pallas as pl
from jax.experimental.pallas import tpu as pltpu
from jax.sharding import PartitionSpec as P

PLANE = ("row", "col")
MIB = 1 << 20


def place(x, y, core):
    return ((x // 2) * 2 + core) * 8 + y * 2 + x % 2


CHIPS = [(x, y, core) for x in range(4) for y in range(4) for core in range(2)]


def shift(value, dx=0, dy=0, other=0):
    pairs = [(place(x, y, c), place((x + dx) % 4, (y + dy) % 4, c ^ other)) for x, y, c in CHIPS]
    return lax.ppermute(value, PLANE, pairs)


def flip_x(value):
    return lax.ppermute(value, PLANE, [(place(x, y, c), place(x ^ 1, y, c)) for x, y, c in CHIPS])


def along_pole(value, step):
    return lax.ppermute(value, "pole", [(z, (z + step) % 8) for z in range(8)])


def pole_pair(value):
    return lax.ppermute(value, "pole", [(z, z ^ 1) for z in range(8)])


def panel_slot(value, j):
    pairs = []
    for x, y, c in CHIPS:
        k = 2 * c + (j ^ (x // 2))
        source = place((y // 2) * 2 + k % 2, 2 * (x % 2) + k // 2, y % 2)
        pairs.append((source, place(x, y, c)))
    return lax.ppermute(value, PLANE, pairs)


def split(value):
    high = value.astype(jnp.bfloat16)
    return high, (value - high.astype(jnp.float32)).astype(jnp.bfloat16)


def mm(a, b, contract=((1,), (0,))):
    return lax.dot_general(a, b, (contract, ((), ())), preferred_element_type=jnp.float32)


def mm3(a_high, a_low, b_high, b_low, contract=((1,), (0,))):
    return mm(a_high, b_high, contract) + (mm(a_high, b_low, contract) + mm(a_low, b_high, contract))


def split_kernel(value, high, low):
    rows = value.shape[0]

    def tile(t, _):
        at = pl.ds(pl.multiple_of(t * TILE, TILE), TILE)
        high[at, :], low[at, :] = split(value[at, :])
        return 0

    lax.fori_loop(0, rows // TILE, tile, 0)


TILE = 256
VMEM = pl.BlockSpec(memory_space=pltpu.VMEM)
SMEM = pl.BlockSpec(memory_space=pltpu.SMEM)


def local(kernel, in_specs, out_shape, flops, moved):
    return pl.pallas_call(
        kernel,
        out_shape=out_shape,
        in_specs=in_specs,
        out_specs=[VMEM] * len(out_shape),
        cost_estimate=pl.CostEstimate(flops=flops, bytes_accessed=moved, transcendentals=0),
        compiler_params=pltpu.CompilerParams(vmem_limit_bytes=16 * MIB),
    )


def split_inverse(inverse):
    rows, depth = inverse.shape
    out_shape = [jax.ShapeDtypeStruct((rows, depth), jnp.bfloat16)] * 2
    return local(split_kernel, [VMEM], out_shape, 4 * rows * depth, 8 * rows * depth)(inverse)


def block_dot(block, rows, a_high, a_low, high, low):
    at = pl.ds(pl.multiple_of(block * rows, rows), rows)
    return mm3(a_high[at, :], a_low[at, :], high[...], low[...])


def first_kernel(info, s0, s1, t0, t1, a_high, a_low, up, down, high, low):
    rows = s0.shape[0]
    middle = rows // 2
    for i, slot in enumerate((s0, s1, t0, t1)):
        at = pl.ds(pl.multiple_of(info[2 + i] * rows, rows), rows)
        keep = (info[6 + i] > 0).astype(jnp.float32)
        high[at, :], low[at, :] = split(slot[...] * keep)

    def block(i, _):
        out = block_dot(info[i], rows, a_high, a_low, high, low)
        to = pl.ds(pl.multiple_of(i * middle, middle), middle)
        up[to, :] = out[:middle]
        down[to, :] = out[middle:]
        return 0

    lax.fori_loop(0, 2, block, 0)


def next_kernel(info, high, low, a_high, a_low, *outs):
    for i, out in enumerate(outs):
        out[...] = block_dot(info[i], out.shape[0], a_high, a_low, high, low)


def first_dot(info, halves, slots):
    rows, width = slots[0].shape
    depth = halves[0].shape[1]
    out_shape = [jax.ShapeDtypeStruct((rows, width), jnp.float32)] * 2
    out_shape += [jax.ShapeDtypeStruct((depth, width), jnp.bfloat16)] * 2
    return local(
        first_kernel, [SMEM] + [VMEM] * 6, out_shape, 12 * rows * depth * width, 8 * rows * (depth + width)
    )(info, *slots, *halves)


def next_dot(info, halves, panel, rows, count):
    depth, width = panel[0].shape
    out_shape = [jax.ShapeDtypeStruct((rows, width), jnp.float32)] * count
    return local(
        next_kernel,
        [SMEM] + [VMEM] * 4,
        out_shape,
        count * 6 * rows * depth * width,
        count * 4 * rows * (depth + width),
    )(info, *panel, *halves)


def corr_kernel(info, weight, total, arrived, own, corr, column, weighted):
    keep = (info[0] > 0).astype(jnp.float32)
    whole = (total[...] + arrived[...]) * keep
    column[...] = -whole
    eighth = whole.shape[0] // 8
    for i in range(8):
        at = (i % 4 * 2 + i // 4) * eighth
        weighted[i * eighth : (i + 1) * eighth, :] = -weight[0] * whole[at : at + eighth, :]
    corr[...] = mm3(*split(own[...]), *split(whole), ((0,), (0,)))


def correction(info, weight, total, arrived, own):
    rows, width = own.shape
    out_shape = [jax.ShapeDtypeStruct((n, width), jnp.float32) for n in (width, rows, rows)]
    return local(corr_kernel, [SMEM] * 2 + [VMEM] * 3, out_shape, 6 * rows * width * width, 24 * rows * width)(
        info, weight, total, arrived, own
    )


def part(value, index, size):
    return lax.dynamic_slice_in_dim(value, index * size, size, 0)


def in_ring_order(value, arrived, me, axis=0):
    size = value.shape[axis]
    rising = [arrived[2], arrived[1], arrived[0], value]
    twice = jnp.concatenate(rising + rising[:3], axis)
    return lax.dynamic_slice_in_dim(twice, (3 - me) * size, 4 * size, axis)


def in_pair_order(value, other, me, axis=0):
    size = value.shape[axis]
    thrice = jnp.concatenate([other, value, other], axis)
    return lax.dynamic_slice_in_dim(thrice, (1 - me) * size, 2 * size, axis)


def on_device(ainv, lfac, dinv, weights, present):
    own = lfac[0]
    rows, width = own.shape
    row, col = lax.axis_index("row"), lax.axis_index("col")
    z = lax.axis_index("pole")
    x_hi, core = row // 2, row % 2
    y, x_lo = col // 2, col % 2
    x = x_hi * 2 + x_lo
    half, quarter = width // 2, width // 8
    weight = weights[0]

    def sibling(v):
        return shift(v, other=1)

    slots = [panel_slot(own, 0), panel_slot(own, 1)]
    order = jnp.stack([2 * core + x_hi, 2 * core + 1 - x_hi, 2 * (1 - core) + x_hi, 2 * (1 - core) + 1 - x_hi])
    keep = jnp.take(present, jnp.concatenate([4 * col + order, (row * 8 + col)[None]]))

    def blocks(d):
        first = 2 * ((y + d) % 4)
        return jnp.stack([first + 1 - x_lo, first + x_lo])

    info = jnp.concatenate([blocks(2), order, keep[:4]]).astype(jnp.int32)
    sides = jnp.concatenate([blocks(1), blocks(3)]).astype(jnp.int32)
    here = blocks(0).astype(jnp.int32)
    tail = keep[4:].astype(jnp.int32)
    dinv_part = lax.dynamic_slice_in_dim(dinv[0], core * half + x * quarter, quarter, 0)
    halves = split_inverse(ainv[0])
    info, sides, here, tail, dinv_part, halves, slots = lax.optimization_barrier(
        (info, sides, here, tail, dinv_part, halves, slots)
    )
    slots += [sibling(s) for s in slots]

    up, down, high, low = first_dot(info, halves, slots)
    panel = (high, low)
    middle = rows // 2
    up, down = shift(up, dy=1), shift(down, dy=-1)
    p1a, p1b, p3a, p3b = next_dot(sides, halves, panel, rows, 4)
    p0a, p0b = next_dot(here, halves, panel, rows, 2)

    def meet(p1, p3, at):
        p1 = jnp.concatenate([p1[:middle] + up[at : at + middle], p1[middle:]])
        p3 = jnp.concatenate([p3[:middle], p3[middle:] + down[at : at + middle]])
        return shift(p1, dy=1), shift(p3, dy=-1)

    from_up, from_down = meet(p1a, p3a, 0)
    arrived = flip_x(p0a + (from_up + from_down))
    from_up, from_down = meet(p1b, p3b, middle)
    total = p0b + (from_up + from_down)
    corr, column, weighted = correction(tail, weights, total, arrived, own)

    pair, four = z % 2, z // 2
    eighth = rows // 8
    steps = (1, 2, 3)
    mine = part(corr, core, half) + sibling(part(corr, 1 - core, half))
    away = [shift(part(mine, (x + k) % 4, quarter), dx=k) for k in steps]
    mine = (part(mine, x, quarter) + away[1]) + (away[0] + away[2])
    dm = part(weighted, pair, middle) + pole_pair(part(weighted, 1 - pair, middle))
    away = [shift(mine, dy=k) for k in steps]
    diagonal = dinv_part + ((mine + away[1]) + (away[0] + away[2]))
    paired = weight * diagonal
    paired = paired + pole_pair(paired)

    away = [along_pole(jnp.concatenate([part(dm, (four + k) % 4, eighth), paired]), 2 * k) for k in steps]
    summed = (jnp.concatenate([part(dm, four, eighth), paired]) + away[1]) + (away[0] + away[2])

    both = jnp.stack([diagonal, summed[eighth:]])
    both = in_ring_order(both, [shift(both, dx=k) for k in steps], x, 1)
    both = in_pair_order(both, sibling(both), core, 1)
    dm = summed[:eighth]
    dm = in_pair_order(dm, pole_pair(dm), pair)
    dm = in_ring_order(dm, [along_pole(dm, 2 * k) for k in steps], four)

    return column[None], both[:1], dm, both[1]


def solution(mesh):
    return jax.shard_map(
        on_device,
        mesh=mesh,
        in_specs=(
            P("pole", "row", "col"),
            P("pole", ("row", "col"), None),
            P("pole", None, None),
            P("pole"),
            P(),
        ),
        out_specs=(
            P("pole", ("row", "col"), None),
            P("pole", None, None),
            P(("row", "col"), None),
            P(),
        ),
        check_vma=False,
    )
```

```python
import jax
import jax.numpy as jnp
from jax import lax
from jax.experimental import pallas as pl
from jax.experimental.pallas import tpu as pltpu
from jax.sharding import PartitionSpec as P

PLANE = ("row", "col")
MIB = 1 << 20


def place(x, y, core):
    return ((x // 2) * 2 + core) * 8 + y * 2 + x % 2


CHIPS = [(x, y, core) for x in range(4) for y in range(4) for core in range(2)]


def shift(value, dx=0, dy=0, other=0):
    pairs = [(place(x, y, c), place((x + dx) % 4, (y + dy) % 4, c ^ other)) for x, y, c in CHIPS]
    return lax.ppermute(value, PLANE, pairs)


def flip_x(value):
    return lax.ppermute(value, PLANE, [(place(x, y, c), place(x ^ 1, y, c)) for x, y, c in CHIPS])


def along_pole(value, step):
    return lax.ppermute(value, "pole", [(z, (z + step) % 8) for z in range(8)])


def pole_pair(value):
    return lax.ppermute(value, "pole", [(z, z ^ 1) for z in range(8)])


def panel_slot(value, j):
    pairs = []
    for x, y, c in CHIPS:
        k = 2 * c + (j ^ (x // 2))
        source = place((y // 2) * 2 + k % 2, 2 * (x % 2) + k // 2, y % 2)
        pairs.append((source, place(x, y, c)))
    return lax.ppermute(value, PLANE, pairs)


def split(value):
    high = value.astype(jnp.bfloat16)
    return high, (value - high.astype(jnp.float32)).astype(jnp.bfloat16)


def mm(a, b, contract=((1,), (0,))):
    return lax.dot_general(a, b, (contract, ((), ())), preferred_element_type=jnp.float32)


def mm3(a_high, a_low, b_high, b_low, contract=((1,), (0,))):
    return mm(a_high, b_high, contract) + (mm(a_high, b_low, contract) + mm(a_low, b_high, contract))


def split_kernel(value, high, low):
    rows = value.shape[0]

    def tile(t, _):
        at = pl.ds(pl.multiple_of(t * TILE, TILE), TILE)
        high[at, :], low[at, :] = split(value[at, :])
        return 0

    lax.fori_loop(0, rows // TILE, tile, 0)


TILE = 256
VMEM = pl.BlockSpec(memory_space=pltpu.VMEM)
SMEM = pl.BlockSpec(memory_space=pltpu.SMEM)


def local(kernel, in_specs, out_shape, flops, moved, scratch=()):
    return pl.pallas_call(
        kernel,
        out_shape=out_shape,
        in_specs=in_specs,
        out_specs=[VMEM] * len(out_shape),
        scratch_shapes=list(scratch),
        cost_estimate=pl.CostEstimate(flops=flops, bytes_accessed=moved, transcendentals=0),
        compiler_params=pltpu.CompilerParams(vmem_limit_bytes=16 * MIB),
    )


def split_inverse(inverse):
    rows, depth = inverse.shape
    out_shape = [jax.ShapeDtypeStruct((rows, depth), jnp.bfloat16)] * 2
    return local(split_kernel, [VMEM], out_shape, 4 * rows * depth, 8 * rows * depth)(inverse)


def block_dot(block, rows, a_high, a_low, high, low):
    at = pl.ds(pl.multiple_of(block * rows, rows), rows)
    return mm3(a_high[at, :], a_low[at, :], high[...], low[...])


def half_dot(block, side, rows, a_high, a_low, high, low):
    depth = high.shape[0]
    at = pl.ds(pl.multiple_of(block * rows, rows), rows)
    over = pl.ds(pl.multiple_of(side * depth, depth), depth)
    return mm3(a_high[at, over], a_low[at, over], high[...], low[...])


def own_kernel(info, s0, s1, a_high, a_low, up, down, high, low):
    rows = s0.shape[0]
    for i, slot in enumerate((s0, s1)):
        at = pl.ds(pl.multiple_of(info[3 + i] * rows, rows), rows)
        keep = (info[5 + i] > 0).astype(jnp.float32)
        high[at, :], low[at, :] = split(slot[...] * keep)
    up[...] = half_dot(info[0], info[2], rows, a_high, a_low, high, low)
    down[...] = half_dot(info[1], info[2], rows, a_high, a_low, high, low)


def rest_kernel(info, t0, t1, up_own, down_own, high_own, low_own, a_high, a_low, up, down, high, low, high_t, low_t):
    rows = t0.shape[0]
    for i, slot in enumerate((t0, t1)):
        at = pl.ds(pl.multiple_of(info[3 + i] * rows, rows), rows)
        keep = (info[5 + i] > 0).astype(jnp.float32)
        high_t[at, :], low_t[at, :] = split(slot[...] * keep)
    side = info[2]
    up[...] = up_own[...] + half_dot(info[0], side, rows, a_high, a_low, high_t, low_t)
    down[...] = down_own[...] + half_dot(info[1], side, rows, a_high, a_low, high_t, low_t)
    here = pl.ds(pl.multiple_of(side * 2 * rows, 2 * rows), 2 * rows)
    there = pl.ds(pl.multiple_of((1 - side) * 2 * rows, 2 * rows), 2 * rows)
    high[here, :], low[here, :] = high_t[...], low_t[...]
    high[there, :], low[there, :] = high_own[...], low_own[...]


def next_kernel(info, high, low, a_high, a_low, *outs):
    for i, out in enumerate(outs):
        out[...] = block_dot(info[i], out.shape[0], a_high, a_low, high, low)


def own_dot(info, halves, slots):
    rows, width = slots[0].shape
    out_shape = [jax.ShapeDtypeStruct((rows, width), jnp.float32)] * 2
    out_shape += [jax.ShapeDtypeStruct((2 * rows, width), jnp.bfloat16)] * 2
    return local(
        own_kernel, [SMEM] + [VMEM] * 4, out_shape, 24 * rows * rows * width, 8 * rows * (2 * rows + 3 * width)
    )(info, *slots, *halves)


def rest_dot(info, halves, slots, done):
    rows, width = slots[0].shape
    out_shape = [jax.ShapeDtypeStruct((rows, width), jnp.float32)] * 2
    out_shape += [jax.ShapeDtypeStruct((4 * rows, width), jnp.bfloat16)] * 2
    scratch = [pltpu.VMEM((2 * rows, width), jnp.bfloat16)] * 2
    return local(
        rest_kernel,
        [SMEM] + [VMEM] * 8,
        out_shape,
        24 * rows * rows * width,
        8 * rows * (2 * rows + 5 * width),
        scratch,
    )(info, *slots, *done, *halves)


def next_dot(info, halves, panel, rows, count):
    depth, width = panel[0].shape
    out_shape = [jax.ShapeDtypeStruct((rows, width), jnp.float32)] * count
    return local(
        next_kernel,
        [SMEM] + [VMEM] * 4,
        out_shape,
        count * 6 * rows * depth * width,
        count * 4 * rows * (depth + width),
    )(info, *panel, *halves)


def turn_kernel(own, other, own_high, own_low, other_high, other_low):
    own_high[...], own_low[...] = split(own[...].T)
    other_high[...], other_low[...] = split(other[...].T)


def turned(own, other):
    rows, width = own.shape
    out_shape = [jax.ShapeDtypeStruct((width, rows), jnp.bfloat16)] * 4
    return local(turn_kernel, [VMEM] * 2, out_shape, 8 * rows * width, 16 * rows * width)(own, other)


def corr_kernel(info, p0, p1, up0, down0, up1, down1, oh, ol, th, tl, corr, sum_own, sum_other):
    first = p0[...] + (up0[...] + down0[...])
    second = p1[...] + (up1[...] + down1[...])
    own_is_first = info[0] == 0
    mine = jnp.where(own_is_first, first, second) * (info[1] > 0).astype(jnp.float32)
    others = jnp.where(own_is_first, second, first) * (info[2] > 0).astype(jnp.float32)
    sum_own[...] = mine
    sum_other[...] = others
    corr[...] = mm3(oh[...], ol[...], *split(mine)) + mm3(th[...], tl[...], *split(others))


def correction(info, *arrays):
    rows, width = arrays[0].shape
    out_shape = [jax.ShapeDtypeStruct((n, width), jnp.float32) for n in (width, rows, rows)]
    return local(
        corr_kernel, [SMEM] + [VMEM] * len(arrays), out_shape, 12 * rows * width * width, 48 * rows * width
    )(info, *arrays)


def column_kernel(weight, mine, arrived, column, weighted):
    whole = mine[...] + arrived[...]
    column[...] = -whole
    eighth = whole.shape[0] // 8
    for i in range(8):
        at = (i % 4 * 2 + i // 4) * eighth
        weighted[i * eighth : (i + 1) * eighth, :] = -weight[0] * whole[at : at + eighth, :]


def inverse_column(weight, mine, arrived):
    rows, width = mine.shape
    out_shape = [jax.ShapeDtypeStruct((rows, width), jnp.float32)] * 2
    return local(column_kernel, [SMEM] + [VMEM] * 2, out_shape, 3 * rows * width, 16 * rows * width)(
        weight, mine, arrived
    )


def part(value, index, size):
    return lax.dynamic_slice_in_dim(value, index * size, size, 0)


def in_ring_order(value, arrived, me, axis=0):
    size = value.shape[axis]
    rising = [arrived[2], arrived[1], arrived[0], value]
    twice = jnp.concatenate(rising + rising[:3], axis)
    return lax.dynamic_slice_in_dim(twice, (3 - me) * size, 4 * size, axis)


def in_pair_order(value, other, me, axis=0):
    size = value.shape[axis]
    thrice = jnp.concatenate([other, value, other], axis)
    return lax.dynamic_slice_in_dim(thrice, (1 - me) * size, 2 * size, axis)


def on_device(ainv, lfac, dinv, weights, present):
    own = lfac[0]
    rows, width = own.shape
    row, col = lax.axis_index("row"), lax.axis_index("col")
    z = lax.axis_index("pole")
    x_hi, core = row // 2, row % 2
    y, x_lo = col // 2, col % 2
    half, quarter = width // 2, width // 8
    weight = weights[0]

    def sibling(v):
        return shift(v, other=1)

    slots = [panel_slot(own, 0), panel_slot(own, 1)]
    order = jnp.stack([2 * core + x_hi, 2 * core + 1 - x_hi, 2 * (1 - core) + x_hi, 2 * (1 - core) + 1 - x_hi])
    keep = jnp.take(present, jnp.concatenate([4 * col + order, row * 8 + jnp.stack([col, col ^ 1])]))

    def block(d, x_lo):
        return 2 * ((y + d) % 4) + x_lo

    far = jnp.stack([block(2, 0), block(2, 1)])
    places = jnp.stack([x_hi, 1 - x_hi])
    info = jnp.concatenate([far, core[None], places, keep[:2]]).astype(jnp.int32)
    rest = jnp.concatenate([far, 1 - core[None], places, keep[2:4]]).astype(jnp.int32)
    straight = jnp.stack([block(1, 1), block(3, 0)]).astype(jnp.int32)
    joined = jnp.stack([block(1, 0), block(3, 1)]).astype(jnp.int32)
    here = jnp.stack([block(0, 0), block(0, 1)]).astype(jnp.int32)
    tail = jnp.concatenate([x_lo[None], keep[4:]]).astype(jnp.int32)
    dinv_part = lax.dynamic_slice_in_dim(dinv[0], core * half + y * quarter, quarter, 0)
    halves = split_inverse(ainv[0])
    info, rest, straight, joined, here, tail, dinv_part, halves, slots = lax.optimization_barrier(
        (info, rest, straight, joined, here, tail, dinv_part, halves, slots)
    )
    others = [sibling(s) for s in slots]

    up, down, high, low = rest_dot(rest, halves, others, own_dot(info, halves, slots))
    panel = (high, low)
    up, down = shift(up, dy=1), shift(down, dy=-1)
    p11, p30 = next_dot(straight, halves, panel, rows, 2)
    up1, down0 = shift(p11, dy=1), shift(p30, dy=-1)
    p10, p31 = next_dot(joined, halves, panel, rows, 2)
    up0, down1 = shift(p10 + up, dy=1), shift(p31 + down, dy=-1)
    p00, p01 = next_dot(here, halves, panel, rows, 2)
    corr, sum_own, sum_other = correction(tail, p00, p01, up0, down0, up1, down1, *turned(own, flip_x(own)))

    pair, four = z % 2, z // 2
    eighth, middle = rows // 8, rows // 2
    column, weighted = inverse_column(weights, sum_own, flip_x(sum_other))
    dm = part(weighted, pair, middle) + pole_pair(part(weighted, 1 - pair, middle))

    steps = (1, 2, 3)
    mine = part(corr, core, half) + sibling(part(corr, 1 - core, half))
    away = [shift(part(mine, (y + k) % 4, quarter), dy=k) for k in steps]
    mine = (part(mine, y, quarter) + away[1]) + (away[0] + away[2])
    away = [shift(mine, dx=k) for k in steps]
    diagonal = dinv_part + ((mine + away[1]) + (away[0] + away[2]))
    paired = weight * diagonal
    paired = paired + pole_pair(paired)

    away = [along_pole(jnp.concatenate([part(dm, (four + k) % 4, eighth), paired]), 2 * k) for k in steps]
    summed = (jnp.concatenate([part(dm, four, eighth), paired]) + away[1]) + (away[0] + away[2])

    both = jnp.stack([diagonal, summed[eighth:]])
    both = in_ring_order(both, [shift(both, dy=k) for k in steps], y, 1)
    both = in_pair_order(both, sibling(both), core, 1)
    dm = summed[:eighth]
    dm = in_pair_order(dm, pole_pair(dm), pair)
    dm = in_ring_order(dm, [along_pole(dm, 2 * k) for k in steps], four)

    return column[None], both[:1], dm, both[1]


def solution(mesh):
    return jax.shard_map(
        on_device,
        mesh=mesh,
        in_specs=(
            P("pole", "row", "col"),
            P("pole", ("row", "col"), None),
            P("pole", None, None),
            P("pole"),
            P(),
        ),
        out_specs=(
            P("pole", ("row", "col"), None),
            P("pole", None, None),
            P(("row", "col"), None),
            P(),
        ),
        check_vma=False,
    )
```

```python
import jax
import jax.numpy as jnp
from jax import lax
from jax.experimental import pallas as pl
from jax.experimental.pallas import tpu as pltpu
from jax.sharding import PartitionSpec as P

PLANE = ("row", "col")
MIB = 1 << 20


def place(x, y, core):
    return ((x // 2) * 2 + core) * 8 + y * 2 + x % 2


CHIPS = [(x, y, core) for x in range(4) for y in range(4) for core in range(2)]


def shift(value, dx=0, dy=0, other=0):
    pairs = [(place(x, y, c), place((x + dx) % 4, (y + dy) % 4, c ^ other)) for x, y, c in CHIPS]
    return lax.ppermute(value, PLANE, pairs)


def flip_x(value):
    return lax.ppermute(value, PLANE, [(place(x, y, c), place(x ^ 1, y, c)) for x, y, c in CHIPS])


def along_pole(value, step):
    return lax.ppermute(value, "pole", [(z, (z + step) % 8) for z in range(8)])


def pole_pair(value):
    return lax.ppermute(value, "pole", [(z, z ^ 1) for z in range(8)])


def panel_slot(value, j):
    pairs = []
    for x, y, c in CHIPS:
        k = 2 * c + (j ^ (x // 2))
        source = place((y // 2) * 2 + k % 2, 2 * (x % 2) + k // 2, y % 2)
        pairs.append((source, place(x, y, c)))
    return lax.ppermute(value, PLANE, pairs)


def split(value):
    high = value.astype(jnp.bfloat16)
    return high, (value - high.astype(jnp.float32)).astype(jnp.bfloat16)


def mm(a, b, contract=((1,), (0,))):
    return lax.dot_general(a, b, (contract, ((), ())), preferred_element_type=jnp.float32)


def mm3(a_high, a_low, b_high, b_low, contract=((1,), (0,))):
    return mm(a_high, b_high, contract) + (mm(a_high, b_low, contract) + mm(a_low, b_high, contract))


def split_kernel(value, high, low):
    rows = value.shape[0]

    def tile(t, _):
        at = pl.ds(pl.multiple_of(t * TILE, TILE), TILE)
        high[at, :], low[at, :] = split(value[at, :])
        return 0

    lax.fori_loop(0, rows // TILE, tile, 0)


TILE = 256
VMEM = pl.BlockSpec(memory_space=pltpu.VMEM)
SMEM = pl.BlockSpec(memory_space=pltpu.SMEM)


def local(kernel, in_specs, out_shape, flops, moved, scratch=()):
    return pl.pallas_call(
        kernel,
        out_shape=out_shape,
        in_specs=in_specs,
        out_specs=[VMEM] * len(out_shape),
        scratch_shapes=list(scratch),
        cost_estimate=pl.CostEstimate(flops=flops, bytes_accessed=moved, transcendentals=0),
        compiler_params=pltpu.CompilerParams(vmem_limit_bytes=16 * MIB),
    )


def split_inverse(inverse):
    rows, depth = inverse.shape
    out_shape = [jax.ShapeDtypeStruct((rows, depth), jnp.bfloat16)] * 2
    return local(split_kernel, [VMEM], out_shape, 4 * rows * depth, 8 * rows * depth)(inverse)


def block_dot(block, rows, a_high, a_low, high, low):
    at = pl.ds(pl.multiple_of(block * rows, rows), rows)
    return mm3(a_high[at, :], a_low[at, :], high[...], low[...])


def half_dot(block, side, rows, a_high, a_low, high, low):
    depth = high.shape[0]
    at = pl.ds(pl.multiple_of(block * rows, rows), rows)
    over = pl.ds(pl.multiple_of(side * depth, depth), depth)
    return mm3(a_high[at, over], a_low[at, over], high[...], low[...])


def own_kernel(info, s0, s1, a_high, a_low, up, down, high, low):
    rows = s0.shape[0]
    for i, slot in enumerate((s0, s1)):
        at = pl.ds(pl.multiple_of(info[3 + i] * rows, rows), rows)
        keep = (info[5 + i] > 0).astype(jnp.float32)
        high[at, :], low[at, :] = split(slot[...] * keep)
    up[...] = half_dot(info[0], info[2], rows, a_high, a_low, high, low)
    down[...] = half_dot(info[1], info[2], rows, a_high, a_low, high, low)


def rest_kernel(info, t0, t1, up_own, down_own, high_own, low_own, a_high, a_low, up, down, high, low, high_t, low_t):
    rows = t0.shape[0]
    for i, slot in enumerate((t0, t1)):
        at = pl.ds(pl.multiple_of(info[3 + i] * rows, rows), rows)
        keep = (info[5 + i] > 0).astype(jnp.float32)
        high_t[at, :], low_t[at, :] = split(slot[...] * keep)
    side = info[2]
    up[...] = up_own[...] + half_dot(info[0], side, rows, a_high, a_low, high_t, low_t)
    down[...] = down_own[...] + half_dot(info[1], side, rows, a_high, a_low, high_t, low_t)
    here = pl.ds(pl.multiple_of(side * 2 * rows, 2 * rows), 2 * rows)
    there = pl.ds(pl.multiple_of((1 - side) * 2 * rows, 2 * rows), 2 * rows)
    high[here, :], low[here, :] = high_t[...], low_t[...]
    high[there, :], low[there, :] = high_own[...], low_own[...]


def next_kernel(info, high, low, a_high, a_low, *outs):
    for i, out in enumerate(outs):
        out[...] = block_dot(info[i], out.shape[0], a_high, a_low, high, low)


def own_dot(info, halves, slots):
    rows, width = slots[0].shape
    out_shape = [jax.ShapeDtypeStruct((rows, width), jnp.float32)] * 2
    out_shape += [jax.ShapeDtypeStruct((2 * rows, width), jnp.bfloat16)] * 2
    return local(
        own_kernel, [SMEM] + [VMEM] * 4, out_shape, 24 * rows * rows * width, 8 * rows * (2 * rows + 3 * width)
    )(info, *slots, *halves)


def rest_dot(info, halves, slots, done):
    rows, width = slots[0].shape
    out_shape = [jax.ShapeDtypeStruct((rows, width), jnp.float32)] * 2
    out_shape += [jax.ShapeDtypeStruct((4 * rows, width), jnp.bfloat16)] * 2
    scratch = [pltpu.VMEM((2 * rows, width), jnp.bfloat16)] * 2
    return local(
        rest_kernel,
        [SMEM] + [VMEM] * 8,
        out_shape,
        24 * rows * rows * width,
        8 * rows * (2 * rows + 5 * width),
        scratch,
    )(info, *slots, *done, *halves)


def next_dot(info, halves, panel, rows, count):
    depth, width = panel[0].shape
    out_shape = [jax.ShapeDtypeStruct((rows, width), jnp.float32)] * count
    return local(
        next_kernel,
        [SMEM] + [VMEM] * 4,
        out_shape,
        count * 6 * rows * depth * width,
        count * 4 * rows * (depth + width),
    )(info, *panel, *halves)


def turn_kernel(own, other, own_high, own_low, other_high, other_low):
    own_high[...], own_low[...] = split(own[...].T)
    other_high[...], other_low[...] = split(other[...].T)


def turned(own, other):
    rows, width = own.shape
    out_shape = [jax.ShapeDtypeStruct((width, rows), jnp.bfloat16)] * 4
    return local(turn_kernel, [VMEM] * 2, out_shape, 8 * rows * width, 16 * rows * width)(own, other)


def corr_kernel(info, p0, p1, up0, down0, up1, down1, oh, ol, th, tl, kept, sent, sum_own, sum_other):
    first = p0[...] + (up0[...] + down0[...])
    second = p1[...] + (up1[...] + down1[...])
    own_is_first = info[0] == 0
    mine = jnp.where(own_is_first, first, second) * (info[1] > 0).astype(jnp.float32)
    others = jnp.where(own_is_first, second, first) * (info[2] > 0).astype(jnp.float32)
    sum_own[...] = mine
    sum_other[...] = others
    corr = mm3(oh[...], ol[...], *split(mine)) + mm3(th[...], tl[...], *split(others))
    half = corr.shape[0] // 2
    first_core = info[3] == 0
    kept[...] = jnp.where(first_core, corr[:half], corr[half:])
    sent[...] = jnp.where(first_core, corr[half:], corr[:half])


def correction(info, *arrays):
    rows, width = arrays[0].shape
    out_shape = [jax.ShapeDtypeStruct((n, width), jnp.float32) for n in (width // 2, width // 2, rows, rows)]
    return local(
        corr_kernel, [SMEM] + [VMEM] * len(arrays), out_shape, 12 * rows * width * width, 48 * rows * width
    )(info, *arrays)


def column_kernel(weight, mine, arrived, column, weighted):
    whole = mine[...] + arrived[...]
    column[...] = -whole
    eighth = whole.shape[0] // 8
    for i in range(8):
        at = (i % 4 * 2 + i // 4) * eighth
        weighted[i * eighth : (i + 1) * eighth, :] = -weight[0] * whole[at : at + eighth, :]


def inverse_column(weight, mine, arrived):
    rows, width = mine.shape
    out_shape = [jax.ShapeDtypeStruct((rows, width), jnp.float32)] * 2
    return local(column_kernel, [SMEM] + [VMEM] * 2, out_shape, 3 * rows * width, 16 * rows * width)(
        weight, mine, arrived
    )


def finish_kernel(core, mine, others, diagonal, dm_diag):
    half = mine.shape[1]
    for side, halves in ((core[0], mine), (1 - core[0], others)):
        at = pl.ds(pl.multiple_of(side * half, half), half)
        diagonal[at, :] = halves[0]
        dm_diag[at, :] = halves[1]


def finish(core, mine, others):
    width = mine.shape[2]
    out_shape = [jax.ShapeDtypeStruct((width, width), jnp.float32)] * 2
    return local(finish_kernel, [SMEM] + [VMEM] * 2, out_shape, 0, 16 * width * width)(core[None], mine, others)


def part(value, index, size):
    return lax.dynamic_slice_in_dim(value, index * size, size, 0)


def in_ring_order(value, arrived, me, axis=0):
    size = value.shape[axis]
    rising = [arrived[2], arrived[1], arrived[0], value]
    twice = jnp.concatenate(rising + rising[:3], axis)
    return lax.dynamic_slice_in_dim(twice, (3 - me) * size, 4 * size, axis)


def in_pair_order(value, other, me, axis=0):
    size = value.shape[axis]
    thrice = jnp.concatenate([other, value, other], axis)
    return lax.dynamic_slice_in_dim(thrice, (1 - me) * size, 2 * size, axis)


def on_device(ainv, lfac, dinv, weights, present):
    own = lfac[0]
    rows, width = own.shape
    row, col = lax.axis_index("row"), lax.axis_index("col")
    z = lax.axis_index("pole")
    x_hi, core = row // 2, row % 2
    y, x_lo = col // 2, col % 2
    half, quarter = width // 2, width // 8
    weight = weights[0]

    def sibling(v):
        return shift(v, other=1)

    slots = [panel_slot(own, 0), panel_slot(own, 1)]
    order = jnp.stack([2 * core + x_hi, 2 * core + 1 - x_hi, 2 * (1 - core) + x_hi, 2 * (1 - core) + 1 - x_hi])
    keep = jnp.take(present, jnp.concatenate([4 * col + order, row * 8 + jnp.stack([col, col ^ 1])]))

    def block(d, x_lo):
        return 2 * ((y + d) % 4) + x_lo

    far = jnp.stack([block(2, 0), block(2, 1)])
    places = jnp.stack([x_hi, 1 - x_hi])
    info = jnp.concatenate([far, core[None], places, keep[:2]]).astype(jnp.int32)
    rest = jnp.concatenate([far, 1 - core[None], places, keep[2:4]]).astype(jnp.int32)
    straight = jnp.stack([block(1, 1), block(3, 0)]).astype(jnp.int32)
    joined = jnp.stack([block(1, 0), block(3, 1), block(0, 0), block(0, 1)]).astype(jnp.int32)
    tail = jnp.concatenate([x_lo[None], keep[4:], core[None]]).astype(jnp.int32)
    dinv_part = lax.dynamic_slice_in_dim(dinv[0], core * half + y * quarter, quarter, 0)
    halves = split_inverse(ainv[0])
    info, rest, straight, joined, tail, dinv_part, halves, slots = lax.optimization_barrier(
        (info, rest, straight, joined, tail, dinv_part, halves, slots)
    )
    others = [sibling(s) for s in slots]

    up, down, high, low = rest_dot(rest, halves, others, own_dot(info, halves, slots))
    panel = (high, low)
    up, down = shift(up, dy=1), shift(down, dy=-1)
    p11, p30 = next_dot(straight, halves, panel, rows, 2)
    up1, down0 = shift(p11, dy=1), shift(p30, dy=-1)
    p10, p31, p00, p01 = next_dot(joined, halves, panel, rows, 4)
    up0, down1 = shift(p10 + up, dy=1), shift(p31 + down, dy=-1)
    kept, sent, sum_own, sum_other = correction(tail, p00, p01, up0, down0, up1, down1, *turned(own, flip_x(own)))

    pair, four = z % 2, z // 2
    eighth, middle = rows // 8, rows // 2
    column, weighted = inverse_column(weights, sum_own, flip_x(sum_other))
    dm = part(weighted, pair, middle) + pole_pair(part(weighted, 1 - pair, middle))

    steps = (1, 2, 3)
    mine = kept + sibling(sent)
    away = [shift(part(mine, (y + k) % 4, quarter), dy=k) for k in steps]
    mine = (part(mine, y, quarter) + away[1]) + (away[0] + away[2])
    away = [shift(mine, dx=k) for k in steps]
    diagonal = dinv_part + ((mine + away[1]) + (away[0] + away[2]))
    paired = weight * diagonal
    paired = paired + pole_pair(paired)

    away = [along_pole(jnp.concatenate([part(dm, (four + k) % 4, eighth), paired]), 2 * k) for k in steps]
    summed = (jnp.concatenate([part(dm, four, eighth), paired]) + away[1]) + (away[0] + away[2])

    both = jnp.stack([diagonal, summed[eighth:]])
    both = in_ring_order(both, [shift(both, dy=k) for k in steps], y, 1)
    diagonal, dm_diag = finish(core, both, sibling(both))
    dm = summed[:eighth]
    dm = in_pair_order(dm, pole_pair(dm), pair)
    dm = in_ring_order(dm, [along_pole(dm, 2 * k) for k in steps], four)

    return column[None], diagonal[None], dm, dm_diag


def solution(mesh):
    return jax.shard_map(
        on_device,
        mesh=mesh,
        in_specs=(
            P("pole", "row", "col"),
            P("pole", ("row", "col"), None),
            P("pole", None, None),
            P("pole"),
            P(),
        ),
        out_specs=(
            P("pole", ("row", "col"), None),
            P("pole", None, None),
            P(("row", "col"), None),
            P(),
        ),
        check_vma=False,
    )
```

```python
import jax
import jax.numpy as jnp
from jax import lax
from jax.experimental import pallas as pl
from jax.experimental.pallas import tpu as pltpu
from jax.sharding import PartitionSpec as P

PLANE = ("row", "col")
MIB = 1 << 20


def place(x, y, core):
    return ((x // 2) * 2 + core) * 8 + y * 2 + x % 2


CHIPS = [(x, y, core) for x in range(4) for y in range(4) for core in range(2)]


def shift(value, dx=0, dy=0, other=0):
    pairs = [(place(x, y, c), place((x + dx) % 4, (y + dy) % 4, c ^ other)) for x, y, c in CHIPS]
    return lax.ppermute(value, PLANE, pairs)


def flip_x(value):
    return lax.ppermute(value, PLANE, [(place(x, y, c), place(x ^ 1, y, c)) for x, y, c in CHIPS])


def along_pole(value, step):
    return lax.ppermute(value, "pole", [(z, (z + step) % 8) for z in range(8)])


def pole_pair(value):
    return lax.ppermute(value, "pole", [(z, z ^ 1) for z in range(8)])


def panel_slot(value, j):
    pairs = []
    for x, y, c in CHIPS:
        k = 2 * c + (j ^ (x // 2))
        source = place((y // 2) * 2 + k % 2, 2 * (x % 2) + k // 2, y % 2)
        pairs.append((source, place(x, y, c)))
    return lax.ppermute(value, PLANE, pairs)


def split(value):
    high = value.astype(jnp.bfloat16)
    return high, (value - high.astype(jnp.float32)).astype(jnp.bfloat16)


def mm(a, b, contract=((1,), (0,))):
    return lax.dot_general(a, b, (contract, ((), ())), preferred_element_type=jnp.float32)


def mm3(a_high, a_low, b_high, b_low, contract=((1,), (0,))):
    return mm(a_high, b_high, contract) + (mm(a_high, b_low, contract) + mm(a_low, b_high, contract))


def split_kernel(value, high, low):
    rows = value.shape[0]

    def tile(t, _):
        at = pl.ds(pl.multiple_of(t * TILE, TILE), TILE)
        high[at, :], low[at, :] = split(value[at, :])
        return 0

    lax.fori_loop(0, rows // TILE, tile, 0)


TILE = 256
VMEM = pl.BlockSpec(memory_space=pltpu.VMEM)
SMEM = pl.BlockSpec(memory_space=pltpu.SMEM)


def local(kernel, in_specs, out_shape, flops, moved, scratch=()):
    return pl.pallas_call(
        kernel,
        out_shape=out_shape,
        in_specs=in_specs,
        out_specs=[VMEM] * len(out_shape),
        scratch_shapes=list(scratch),
        cost_estimate=pl.CostEstimate(flops=flops, bytes_accessed=moved, transcendentals=0),
        compiler_params=pltpu.CompilerParams(vmem_limit_bytes=16 * MIB),
    )


def split_inverse(inverse):
    rows, depth = inverse.shape
    out_shape = [jax.ShapeDtypeStruct((rows, depth), jnp.bfloat16)] * 2
    return local(split_kernel, [VMEM], out_shape, 4 * rows * depth, 8 * rows * depth)(inverse)


def block_dot(block, rows, a_high, a_low, high, low):
    at = pl.ds(pl.multiple_of(block * rows, rows), rows)
    return mm3(a_high[at, :], a_low[at, :], high[...], low[...])


def half_dot(block, side, rows, a_high, a_low, high, low):
    depth = high.shape[0]
    at = pl.ds(pl.multiple_of(block * rows, rows), rows)
    over = pl.ds(pl.multiple_of(side * depth, depth), depth)
    return mm3(a_high[at, over], a_low[at, over], high[...], low[...])


def own_kernel(info, s0, s1, a_high, a_low, up, down, high, low):
    rows = s0.shape[0]
    for i, slot in enumerate((s0, s1)):
        at = pl.ds(pl.multiple_of(info[3 + i] * rows, rows), rows)
        keep = (info[5 + i] > 0).astype(jnp.float32)
        high[at, :], low[at, :] = split(slot[...] * keep)
    up[...] = half_dot(info[0], info[2], rows, a_high, a_low, high, low)
    down[...] = half_dot(info[1], info[2], rows, a_high, a_low, high, low)


def rest_kernel(info, t0, t1, up_own, down_own, high_own, low_own, a_high, a_low, up, down, high, low, high_t, low_t):
    rows = t0.shape[0]
    for i, slot in enumerate((t0, t1)):
        at = pl.ds(pl.multiple_of(info[3 + i] * rows, rows), rows)
        keep = (info[5 + i] > 0).astype(jnp.float32)
        high_t[at, :], low_t[at, :] = split(slot[...] * keep)
    side = info[2]
    up[...] = up_own[...] + half_dot(info[0], side, rows, a_high, a_low, high_t, low_t)
    down[...] = down_own[...] + half_dot(info[1], side, rows, a_high, a_low, high_t, low_t)
    here = pl.ds(pl.multiple_of(side * 2 * rows, 2 * rows), 2 * rows)
    there = pl.ds(pl.multiple_of((1 - side) * 2 * rows, 2 * rows), 2 * rows)
    high[here, :], low[here, :] = high_t[...], low_t[...]
    high[there, :], low[there, :] = high_own[...], low_own[...]


def next_kernel(info, high, low, a_high, a_low, *outs):
    for i, out in enumerate(outs):
        out[...] = block_dot(info[i], out.shape[0], a_high, a_low, high, low)


def own_dot(info, halves, slots):
    rows, width = slots[0].shape
    out_shape = [jax.ShapeDtypeStruct((rows, width), jnp.float32)] * 2
    out_shape += [jax.ShapeDtypeStruct((2 * rows, width), jnp.bfloat16)] * 2
    return local(
        own_kernel, [SMEM] + [VMEM] * 4, out_shape, 24 * rows * rows * width, 8 * rows * (2 * rows + 3 * width)
    )(info, *slots, *halves)


def rest_dot(info, halves, slots, done):
    rows, width = slots[0].shape
    out_shape = [jax.ShapeDtypeStruct((rows, width), jnp.float32)] * 2
    out_shape += [jax.ShapeDtypeStruct((4 * rows, width), jnp.bfloat16)] * 2
    scratch = [pltpu.VMEM((2 * rows, width), jnp.bfloat16)] * 2
    return local(
        rest_kernel,
        [SMEM] + [VMEM] * 8,
        out_shape,
        24 * rows * rows * width,
        8 * rows * (2 * rows + 5 * width),
        scratch,
    )(info, *slots, *done, *halves)


def next_dot(info, halves, panel, rows, count):
    depth, width = panel[0].shape
    out_shape = [jax.ShapeDtypeStruct((rows, width), jnp.float32)] * count
    return local(
        next_kernel,
        [SMEM] + [VMEM] * 4,
        out_shape,
        count * 6 * rows * depth * width,
        count * 4 * rows * (depth + width),
    )(info, *panel, *halves)


def join_kernel(p_up, up, p_down, down, for_up, for_down):
    for_up[...] = p_up[...] + up[...]
    for_down[...] = p_down[...] + down[...]


def join(*arrays):
    rows, width = arrays[0].shape
    out_shape = [jax.ShapeDtypeStruct((rows, width), jnp.float32)] * 2
    return local(join_kernel, [VMEM] * 4, out_shape, 2 * rows * width, 24 * rows * width)(*arrays)


def turn_kernel(own, other, own_high, own_low, other_high, other_low):
    own_high[...], own_low[...] = split(own[...].T)
    other_high[...], other_low[...] = split(other[...].T)


def turned(own, other):
    rows, width = own.shape
    out_shape = [jax.ShapeDtypeStruct((width, rows), jnp.bfloat16)] * 4
    return local(turn_kernel, [VMEM] * 2, out_shape, 8 * rows * width, 16 * rows * width)(own, other)


def corr_kernel(info, p0, p1, up0, down0, up1, down1, oh, ol, th, tl, kept, sent, sum_own, sum_other):
    first = p0[...] + (up0[...] + down0[...])
    second = p1[...] + (up1[...] + down1[...])
    own_is_first = info[0] == 0
    mine = jnp.where(own_is_first, first, second) * (info[1] > 0).astype(jnp.float32)
    others = jnp.where(own_is_first, second, first) * (info[2] > 0).astype(jnp.float32)
    sum_own[...] = mine
    sum_other[...] = others
    corr = mm3(oh[...], ol[...], *split(mine)) + mm3(th[...], tl[...], *split(others))
    half = corr.shape[0] // 2
    first_core = info[3] == 0
    kept[...] = jnp.where(first_core, corr[:half], corr[half:])
    sent[...] = jnp.where(first_core, corr[half:], corr[:half])


def correction(info, *arrays):
    rows, width = arrays[0].shape
    out_shape = [jax.ShapeDtypeStruct((n, width), jnp.float32) for n in (width // 2, width // 2, rows, rows)]
    return local(
        corr_kernel, [SMEM] + [VMEM] * len(arrays), out_shape, 12 * rows * width * width, 48 * rows * width
    )(info, *arrays)


def column_kernel(weight, mine, arrived, column, weighted):
    whole = mine[...] + arrived[...]
    column[...] = -whole
    eighth = whole.shape[0] // 8
    for i in range(8):
        at = (i % 4 * 2 + i // 4) * eighth
        weighted[i * eighth : (i + 1) * eighth, :] = -weight[0] * whole[at : at + eighth, :]


def inverse_column(weight, mine, arrived):
    rows, width = mine.shape
    out_shape = [jax.ShapeDtypeStruct((rows, width), jnp.float32)] * 2
    return local(column_kernel, [SMEM] + [VMEM] * 2, out_shape, 3 * rows * width, 16 * rows * width)(
        weight, mine, arrived
    )


def finish_kernel(core, mine, others, diagonal, dm_diag):
    half = mine.shape[1]
    for side, halves in ((core[0], mine), (1 - core[0], others)):
        at = pl.ds(pl.multiple_of(side * half, half), half)
        diagonal[at, :] = halves[0]
        dm_diag[at, :] = halves[1]


def finish(core, mine, others):
    width = mine.shape[2]
    out_shape = [jax.ShapeDtypeStruct((width, width), jnp.float32)] * 2
    return local(finish_kernel, [SMEM] + [VMEM] * 2, out_shape, 0, 16 * width * width)(core[None], mine, others)


def part(value, index, size):
    return lax.dynamic_slice_in_dim(value, index * size, size, 0)


def in_ring_order(value, arrived, me, axis=0):
    size = value.shape[axis]
    rising = [arrived[2], arrived[1], arrived[0], value]
    twice = jnp.concatenate(rising + rising[:3], axis)
    return lax.dynamic_slice_in_dim(twice, (3 - me) * size, 4 * size, axis)


def in_pair_order(value, other, me, axis=0):
    size = value.shape[axis]
    thrice = jnp.concatenate([other, value, other], axis)
    return lax.dynamic_slice_in_dim(thrice, (1 - me) * size, 2 * size, axis)


def on_device(ainv, lfac, dinv, weights, present):
    own = lfac[0]
    rows, width = own.shape
    row, col = lax.axis_index("row"), lax.axis_index("col")
    z = lax.axis_index("pole")
    x_hi, core = row // 2, row % 2
    y, x_lo = col // 2, col % 2
    half, quarter = width // 2, width // 8
    weight = weights[0]

    def sibling(v):
        return shift(v, other=1)

    slots = [panel_slot(own, 0), panel_slot(own, 1)]
    order = jnp.stack([2 * core + x_hi, 2 * core + 1 - x_hi, 2 * (1 - core) + x_hi, 2 * (1 - core) + 1 - x_hi])
    keep = jnp.take(present, jnp.concatenate([4 * col + order, row * 8 + jnp.stack([col, col ^ 1])]))

    def block(d, x_lo):
        return 2 * ((y + d) % 4) + x_lo

    far = jnp.stack([block(2, 0), block(2, 1)])
    places = jnp.stack([x_hi, 1 - x_hi])
    info = jnp.concatenate([far, core[None], places, keep[:2]]).astype(jnp.int32)
    rest = jnp.concatenate([far, 1 - core[None], places, keep[2:4]]).astype(jnp.int32)
    straight = jnp.stack([block(1, 1), block(3, 0)]).astype(jnp.int32)
    joined = jnp.stack([block(1, 0), block(3, 1), block(0, 0), block(0, 1)]).astype(jnp.int32)
    tail = jnp.concatenate([x_lo[None], keep[4:], core[None]]).astype(jnp.int32)
    dinv_part = lax.dynamic_slice_in_dim(dinv[0], core * half + y * quarter, quarter, 0)
    halves = split_inverse(ainv[0])
    info, rest, straight, joined, tail, dinv_part, halves, slots = lax.optimization_barrier(
        (info, rest, straight, joined, tail, dinv_part, halves, slots)
    )
    others = [sibling(s) for s in slots]

    up, down, high, low = rest_dot(rest, halves, others, own_dot(info, halves, slots))
    panel = (high, low)
    up, down = shift(up, dy=1), shift(down, dy=-1)
    p11, p30 = next_dot(straight, halves, panel, rows, 2)
    up1, down0 = shift(p11, dy=1), shift(p30, dy=-1)
    p10, p31, p00, p01 = next_dot(joined, halves, panel, rows, 4)
    for_up, for_down = join(p10, up, p31, down)
    up0, down1 = shift(for_up, dy=1), shift(for_down, dy=-1)
    kept, sent, sum_own, sum_other = correction(tail, p00, p01, up0, down0, up1, down1, *turned(own, flip_x(own)))

    pair, four = z % 2, z // 2
    eighth, middle = rows // 8, rows // 2
    column, weighted = inverse_column(weights, sum_own, flip_x(sum_other))
    dm = part(weighted, pair, middle) + pole_pair(part(weighted, 1 - pair, middle))

    steps = (1, 2, 3)
    mine = kept + sibling(sent)
    away = [shift(part(mine, (y + k) % 4, quarter), dy=k) for k in steps]
    mine = (part(mine, y, quarter) + away[1]) + (away[0] + away[2])
    away = [shift(mine, dx=k) for k in steps]
    diagonal = dinv_part + ((mine + away[1]) + (away[0] + away[2]))
    paired = weight * diagonal
    paired = paired + pole_pair(paired)

    away = [along_pole(jnp.concatenate([part(dm, (four + k) % 4, eighth), paired]), 2 * k) for k in steps]
    summed = (jnp.concatenate([part(dm, four, eighth), paired]) + away[1]) + (away[0] + away[2])

    both = jnp.stack([diagonal, summed[eighth:]])
    both = in_ring_order(both, [shift(both, dy=k) for k in steps], y, 1)
    diagonal, dm_diag = finish(core, both, sibling(both))
    dm = summed[:eighth]
    dm = in_pair_order(dm, pole_pair(dm), pair)
    dm = in_ring_order(dm, [along_pole(dm, 2 * k) for k in steps], four)

    return column[None], diagonal[None], dm, dm_diag


def solution(mesh):
    return jax.shard_map(
        on_device,
        mesh=mesh,
        in_specs=(
            P("pole", "row", "col"),
            P("pole", ("row", "col"), None),
            P("pole", None, None),
            P("pole"),
            P(),
        ),
        out_specs=(
            P("pole", ("row", "col"), None),
            P("pole", None, None),
            P(("row", "col"), None),
            P(),
        ),
        check_vma=False,
    )
```
